32 devices in a mesh: row: 4 (over y, core), col: 8 (over z, x).
Axes of the slice: x: 2, y: 2, z: 4, core: 2. Of those that a mesh axis runs over, the one named last changes fastest.
Arguments:
- rhs: float32 [512, 4096], P('col', 'row'), may hold values from -6 to 6
- couple_prev: float32 [4096, 1024], P('row'), may hold values from -0.1875 to 0.1875
- diag_inverse: float32 [4096, 1024], P('row'), may hold values from -2 to 2
- coupling: bfloat16 [384, 16, 128], P(('row', 'col')), may hold values from -0.5 to 0.5
- pair_block: int32 [384], P(('row', 'col')), may hold values from 0 to 31, as said below
- pair_tile: int32 [384], P(('row', 'col')), may hold values from 0 to 2
- pair_count: int32 [32], P(('row', 'col')), may hold values from 8 to 12, as said below
- owner_slot: int32 [4, 24], P('row'), may hold values from 0 to 23, each once within a row
- schur: bfloat16 [1536, 32768], P('row', 'col'), may hold values from -6 to 6
- surface_factor: bfloat16 [512, 32768], P(None, 'col'), may hold values from -0.125 to 0.125
Outputs:
- updated: bfloat16 [1536, 32768], P('row', 'col')
The draws below stay inside these ranges and needn't reach their ends.
Inputs may be any that keep to these rules, and one draw needn't show every extreme that they name: Among the first pair_count entries of one owner, at most 3 name blocks whose block-row group pair_block // 8 is the same; some owner has exactly 3 from one group. `pair_count`: some owner has 12 live coupling tiles.
All inputs are finite; a program needn't handle non-finite values.
Results may differ from the reference program's by a relative error of at most 0.0055.
Values may be sent and summed in bfloat16 or wider, within the bound.
A program may use at most 128 MiB of HBM per device.

```python
import jax
import jax.numpy as jnp
from jax import lax

NB = 1024
BLK = 128
NRHS = 512
TILE = 16
TPD = 3
KCAP = 12
CAP = 3
NS = 4096
NSURF = 32768
TPR = 24
SR = 384
N_ROW = 4
N_COL = 8


def pair_lists(key):
    owners = N_ROW * N_COL
    base = jax.random.fold_in(key, 4099)
    keys = jax.random.split(base, 6)
    least = 2 * KCAP // 3
    count = jax.random.randint(keys[0], (owners,), least, KCAP + 1)
    full = jax.random.randint(keys[1], (owners,), 0, 8) == 0
    forced = jax.random.randint(keys[2], (), 0, owners)
    full = full | (jnp.arange(owners) == forced)
    count = jnp.where(full, KCAP, count)
    lowest = (forced + 1) % owners
    count = jnp.where(jnp.arange(owners) == lowest, least, count).astype(jnp.int32)
    row_keys = jax.random.split(keys[3], owners)
    others = jax.vmap(lambda k: jax.random.permutation(k, N_ROW - 1))(row_keys) + 1
    offsets = jnp.concatenate([jnp.zeros((owners, 1), jnp.int32), others.astype(jnp.int32)], axis=1)
    group = jnp.arange(KCAP) // CAP
    owner_row = jnp.arange(owners) // N_COL
    source = (owner_row[:, None] + offsets[:, group]) % N_ROW
    order_keys = jax.random.split(keys[4], owners)
    order = jax.vmap(lambda k: jax.random.permutation(k, KCAP))(order_keys)
    source = jnp.take_along_axis(source, order, axis=1)
    local = jax.random.randint(keys[5], (owners, KCAP), 0, NB // BLK)
    blocks = (source * (NB // BLK) + local).astype(jnp.int32)
    tiles = jax.random.randint(jax.random.fold_in(keys[5], 1), (owners, KCAP), 0, TPD).astype(jnp.int32)
    return (blocks.reshape(-1), tiles.reshape(-1), count)


def draw_pair_block(key, part):
    return pair_lists(key)[0]


def draw_pair_tile(key, part):
    return pair_lists(key)[1]


def draw_pair_count(key, part):
    return pair_lists(key)[2]


def draw_diag_inverse(key, part):
    total = NB * N_ROW
    first, second = jax.random.split(jax.random.fold_in(key, 11))
    spread = jax.random.normal(first, (total, NB), jnp.float32) * (0.3 / NB ** 0.5)
    middle = jax.random.uniform(second, (total,), jnp.float32, 0.75, 1.25)
    eye = (jnp.arange(total)[:, None] % NB == jnp.arange(NB)[None, :]).astype(jnp.float32)
    return spread + eye * middle[:, None]


def block_scale(rng, shape, cuts, low, largest):
    def one(axis_at, parts):
        steps = jax.random.uniform(jax.random.fold_in(jax.random.fold_in(rng, 6), axis_at), (parts,), jnp.float32, low / len(cuts), largest / len(cuts))
        return jnp.repeat(jnp.exp(steps), shape[axis_at] // parts).reshape((-1,) + (1,) * (len(shape) - axis_at - 1))

    gain = one(*cuts[0])
    for cut in cuts[1:]:
        gain = gain * one(*cut)
    return gain


def centred(rng, shape, deviation, limit, cuts=(), kind=jnp.bfloat16):
    loudness = block_scale(rng, shape, cuts, -0.22, 0.18) if cuts else 1.0
    values = jax.random.normal(rng, shape, jnp.float32) * deviation * loudness
    return jnp.minimum(jnp.maximum(values, -limit), limit).astype(kind)


def setup_inputs(seed: int = 0) -> dict:
    key_of = jax.random.split(jax.random.key(seed), 11)
    rhs = centred(key_of[0], (NRHS, NS), 1.0, 6.0, ((0, 8), (1, 4)), jnp.float32)
    couple_prev = centred(key_of[1], (NS, NB), NB ** -0.5, 0.1875, ((0, 4),), jnp.float32)
    diag_inverse = draw_diag_inverse(jax.random.fold_in(key_of[10], 71), 0)
    coupling = centred(key_of[3], (N_ROW * N_COL * KCAP, TILE, BLK), BLK ** -0.5, 0.5, ((0, 32),))
    pair_block = draw_pair_block(jax.random.fold_in(key_of[10], 71), 0)
    pair_tile = draw_pair_tile(jax.random.fold_in(key_of[10], 71), 0)
    pair_count = draw_pair_count(jax.random.fold_in(key_of[10], 71), 0)
    owner_slot = jax.vmap(lambda own: jax.random.permutation(own, TPR))(jax.random.split(key_of[7], N_ROW)).reshape((N_ROW, TPR)).astype(jnp.int32)
    schur = centred(key_of[8], (N_ROW * SR, NSURF), 1.0, 6.0, ((0, 4), (1, 8)))
    surface_factor = centred(key_of[9], (NRHS, NSURF), (4 * NRHS) ** -0.5, 0.125, ((1, 8),))
    return {"rhs": rhs, "couple_prev": couple_prev, "diag_inverse": diag_inverse, "coupling": coupling, "pair_block": pair_block, "pair_tile": pair_tile, "pair_count": pair_count, "owner_slot": owner_slot, "schur": schur, "surface_factor": surface_factor}


def owner_update(blocks, tiles, count, tiles_data, sol_blocks):
    hi = lax.Precision.HIGHEST
    picked = jnp.take(sol_blocks, blocks, axis=1)
    product = jnp.einsum("kib,rkb->kir", tiles_data.astype(jnp.float32), picked.astype(jnp.float32), precision=hi)
    live = jnp.arange(KCAP) < count
    weight = ((tiles[None, :] == jnp.arange(TPD)[:, None]) & live[None, :]).astype(jnp.float32)
    return jnp.einsum("tk,kir->tir", weight, product, precision=hi).astype(jnp.bfloat16)


def reference(rhs, couple_prev, diag_inverse, coupling, pair_block, pair_tile, pair_count, owner_slot, schur, surface_factor):
    hi = lax.Precision.HIGHEST
    pieces = []
    previous = None
    for block_row in range(N_ROW):
        right = rhs[:, block_row * NB:(block_row + 1) * NB]
        lower = couple_prev[block_row * NB:(block_row + 1) * NB]
        inverse = diag_inverse[block_row * NB:(block_row + 1) * NB]
        if block_row > 0:
            right = right - jnp.dot(previous, lower, precision=hi, preferred_element_type=jnp.float32)
        previous = jnp.dot(right, inverse, precision=hi, preferred_element_type=jnp.float32)
        pieces.append(previous)
    solution = jnp.concatenate(pieces, axis=1).astype(jnp.bfloat16)
    sol_blocks = solution.reshape(NRHS, NS // BLK, BLK)
    owners = N_ROW * N_COL

    def one_owner(items):
        return owner_update(items[0], items[1], items[2], items[3], sol_blocks)

    update = lax.map(one_owner, (pair_block.reshape(owners, KCAP), pair_tile.reshape(owners, KCAP), pair_count, coupling.reshape(owners, KCAP, TILE, BLK)))
    update = update.reshape(N_ROW, TPR, TILE, NRHS)

    def one_group(items):
        rows_all, slots, slab = items
        rows = jnp.take(rows_all, slots, axis=0).reshape(SR, NRHS)
        change = jnp.dot(rows, surface_factor, preferred_element_type=jnp.float32)
        return (slab.astype(jnp.float32) - change).astype(jnp.bfloat16)

    result = lax.map(one_group, (update, owner_slot, schur.reshape(N_ROW, SR, NSURF)))
    return result.reshape(N_ROW * SR, NSURF)
```

```python
import functools

import jax
import jax.numpy as jnp
from jax import lax
from jax.experimental import pallas as pl
from jax.experimental.pallas import tpu as pltpu
from jax.sharding import PartitionSpec as P

CAP = 3
F32 = jnp.float32
BF16 = jnp.bfloat16
NT = (((1,), (1,)), ((), ()))


def dot(left, right):
    return jnp.dot(left, right, preferred_element_type=F32)


def halves(value):
    high = value.astype(BF16)
    return high, (value - high.astype(F32)).astype(BF16)


def kernel(
    n_rows,
    n_cols,
    rhs,
    couple_hbm,
    inverse_hbm,
    coupling,
    block_ref,
    tile_ref,
    count_ref,
    slot_ref,
    out,
    couple,
    inverse,
    couple_hi,
    couple_lo,
    inverse_hi,
    inverse_lo,
    chunks,
    gathered,
    dense,
    order,
    solved,
    before,
    right,
    partial,
    arrived,
    turned,
    load_sem,
    swap_send,
    swap_recv,
    share_send,
    share_recv,
    hop_sem,
    part_send,
    part_recv,
    turn_send,
    turn_recv,
):
    my_row = lax.axis_index("row")
    my_col = lax.axis_index("col")
    cols, width = rhs.shape
    held, tile, blk = coupling.shape
    per_row = width // blk
    tpr = slot_ref.shape[1]
    tpd = tpr // n_cols
    group = tpr * tile

    load_inverse = pltpu.make_async_copy(inverse_hbm, inverse, load_sem.at[0])
    load_couple = pltpu.make_async_copy(couple_hbm, couple, load_sem.at[1])
    load_inverse.start()
    load_couple.start()

    def row_peer(step):
        return {"row": lax.rem(my_row + step, n_rows)}

    def col_peer(step):
        return {"col": lax.rem(my_col + step, n_cols)}

    barrier = pltpu.get_barrier_semaphore()
    for step in range(1, n_rows):
        pl.semaphore_signal(
            barrier, inc=1, device_id=row_peer(step), device_id_type=pl.DeviceIdType.MESH
        )
    for step in range(1, n_cols):
        pl.semaphore_signal(
            barrier, inc=1, device_id=col_peer(step), device_id_type=pl.DeviceIdType.MESH
        )

    count = count_ref[0]
    keys, codes = [], []
    sources = []
    for k in range(held):
        block = block_ref[k]
        source = lax.div(block, per_row)
        rank = jnp.int32(0)
        for j in range(k):
            rank = rank + jnp.where(sources[j] == source, 1, 0)
        sources.append(jnp.where(k < count, source, -1))
        keys.append(jnp.where(k < count, source * CAP + rank, -1))
        codes.append(tile_ref[k] * per_row + block - source * per_row)
    lines = lax.broadcasted_iota(jnp.int32, (tile, blk), 0)
    for r in range(n_rows):
        marks = jnp.full((tile, blk), -1, jnp.int32)
        for s in range(CAP):
            place, code = jnp.int32(0), jnp.int32(-1)
            for k in range(held):
                hit = keys[k] == r * CAP + s
                place = jnp.where(hit, k, place)
                code = jnp.where(hit, codes[k], code)
            chunks[r, s * tile : (s + 1) * tile, :] = coupling[place]
            marks = jnp.where(lines == s, code, marks)
        chunks[r, CAP * tile : (CAP + 1) * tile, :] = marks.astype(F32).astype(BF16)
    gathered[my_col, my_row] = chunks[my_row]

    pl.semaphore_wait(barrier, n_rows + n_cols - 2)

    swaps = []
    for step in range(1, n_rows):
        swap = pltpu.make_async_remote_copy(
            src_ref=chunks.at[lax.rem(my_row + step, n_rows)],
            dst_ref=gathered.at[my_col, my_row],
            send_sem=swap_send.at[step],
            recv_sem=swap_recv.at[step],
            device_id=row_peer(step),
            device_id_type=pl.DeviceIdType.MESH,
        )
        swap.start()
        swaps.append(swap)

    load_inverse.wait()
    high, low = halves(inverse[...])
    inverse_hi[...] = high
    inverse_lo[...] = low
    load_couple.wait()

    @pl.when(my_row > 0)
    def _():
        high, low = halves(couple[...])
        couple_hi[...] = high
        couple_lo[...] = low

    for swap in swaps:
        swap.wait()
    shares = []
    for step in range(1, n_cols):
        share = pltpu.make_async_remote_copy(
            src_ref=gathered.at[my_col],
            dst_ref=gathered.at[my_col],
            send_sem=share_send.at[step],
            recv_sem=share_recv.at[step],
            device_id=col_peer(step),
            device_id_type=pl.DeviceIdType.MESH,
        )
        share.start()
        shares.append(share)

    hop = pltpu.make_async_remote_copy(
        src_ref=solved,
        dst_ref=before,
        send_sem=hop_sem.at[0],
        recv_sem=hop_sem.at[1],
        device_id=row_peer(1),
        device_id_type=pl.DeviceIdType.MESH,
    )

    def chain():
        right[...] = rhs[...]

        @pl.when(my_row > 0)
        def _():
            hop.wait_recv()
            known = before[...]
            right[...] = rhs[...] - (dot(known, couple_hi[...]) + dot(known, couple_lo[...]))

        high, low = halves(right[...])
        both = dot(jnp.concatenate([high, low], axis=0), inverse_hi[...])
        solved[...] = (both[:cols] + both[cols:] + dot(high, inverse_lo[...])).astype(BF16)

    @pl.when(my_row < n_rows - 1)
    def _():
        chain()
        hop.start()

    for share in shares:
        share.wait()

    def spread(index, _):
        c = index // n_rows
        r = index % n_rows
        marks = gathered[c, r, CAP * tile : (CAP + 1) * tile, :].astype(F32)
        tiles = [gathered[c, r, s * tile : (s + 1) * tile, :] for s in range(CAP)]
        where = [
            jnp.broadcast_to(marks[s : s + 1, :], (tile, blk)).astype(BF16) for s in range(CAP)
        ]
        base = (r * n_cols + c) * (tpd * tile)
        zero = jnp.zeros((tile, blk), BF16)
        for t in range(tpd):
            for j in range(per_row):
                total = zero
                for s in range(CAP):
                    total = total + jnp.where(where[s] == t * per_row + j, tiles[s], zero)
                dense[
                    pl.ds(pl.multiple_of(base + t * tile, tile), tile), j * blk : (j + 1) * blk
                ] = total
        return 0

    lax.fori_loop(0, n_rows * n_cols, spread, 0)

    ahead = lax.broadcasted_iota(jnp.int32, (tile, group), 1)
    down = lax.broadcasted_iota(jnp.int32, (tile, group), 0)
    for i in range(tpr):
        same = ahead == slot_ref[0, i] * tile + down
        order[i * tile : (i + 1) * tile, :] = jnp.where(same, 1.0, 0.0).astype(BF16)

    @pl.when(my_row == n_rows - 1)
    def _():
        chain()

    known = solved[...]
    for r in range(n_rows):
        partial[r] = lax.dot_general(
            known, dense[r * group : (r + 1) * group, :], NT, preferred_element_type=F32
        ).astype(BF16)

    parts = []
    for step in range(1, n_rows):
        part = pltpu.make_async_remote_copy(
            src_ref=partial.at[lax.rem(my_row + step, n_rows)],
            dst_ref=arrived.at[step],
            send_sem=part_send.at[step],
            recv_sem=part_recv.at[step],
            device_id=row_peer(step),
            device_id_type=pl.DeviceIdType.MESH,
        )
        part.start()
        parts.append(part)
    total = partial[my_row].astype(F32)
    for step in range(1, n_rows):
        parts[step - 1].wait_recv()
        total = total + arrived[step].astype(F32)
    mine = pl.ds(pl.multiple_of(my_col * cols, cols), cols)
    turned[mine, :] = total.astype(BF16)

    turns = []
    for step in range(1, n_cols):
        turn = pltpu.make_async_remote_copy(
            src_ref=turned.at[mine],
            dst_ref=turned.at[mine],
            send_sem=turn_send.at[step],
            recv_sem=turn_recv.at[step],
            device_id=col_peer(step),
            device_id_type=pl.DeviceIdType.MESH,
        )
        turn.start()
        turns.append(turn)
    for turn in turns:
        turn.wait_recv()
    out[...] = lax.dot_general(
        order[...], turned[...], NT, preferred_element_type=F32
    ).astype(BF16)

    for copy in parts + turns:
        copy.wait_send()

    @pl.when(my_row < n_rows - 1)
    def _():
        hop.wait_send()


def shards(
    n_rows,
    n_cols,
    rhs,
    couple_prev,
    diag_inverse,
    coupling,
    pair_block,
    pair_tile,
    pair_count,
    owner_slot,
    schur,
    surface_factor,
):
    cols, width = rhs.shape
    held, tile, blk = coupling.shape
    group = owner_slot.shape[1] * tile
    chunk = (CAP + 1) * tile
    dma = pltpu.SemaphoreType.DMA
    vmem = pl.BlockSpec(memory_space=pltpu.VMEM)
    smem = pl.BlockSpec(memory_space=pltpu.SMEM)
    hbm = pl.BlockSpec(memory_space=pl.ANY)
    scratch = [
        pltpu.VMEM((width, width), F32),
        pltpu.VMEM((width, width), F32),
        pltpu.VMEM((width, width), BF16),
        pltpu.VMEM((width, width), BF16),
        pltpu.VMEM((width, width), BF16),
        pltpu.VMEM((width, width), BF16),
        pltpu.VMEM((n_rows, chunk, blk), BF16),
        pltpu.VMEM((n_cols, n_rows, chunk, blk), BF16),
        pltpu.VMEM((n_rows * group, width), BF16),
        pltpu.VMEM((group, group), BF16),
        pltpu.VMEM((cols, width), BF16),
        pltpu.VMEM((cols, width), BF16),
        pltpu.VMEM((cols, width), F32),
        pltpu.VMEM((n_rows, cols, group), BF16),
        pltpu.VMEM((n_rows, cols, group), BF16),
        pltpu.VMEM((n_cols * cols, group), BF16),
        dma((2,)),
        dma((n_rows,)),
        dma((n_rows,)),
        dma((n_cols,)),
        dma((n_cols,)),
        dma((2,)),
        dma((n_rows,)),
        dma((n_rows,)),
        dma((n_cols,)),
        dma((n_cols,)),
    ]
    planned = 16 * width * width + 2 * n_rows * group * width + 2 * n_cols * n_rows * chunk * blk
    rows_w = pl.pallas_call(
        functools.partial(kernel, n_rows, n_cols),
        out_shape=jax.ShapeDtypeStruct((group, n_cols * cols), BF16),
        in_specs=[vmem, hbm, hbm, vmem, smem, smem, smem, smem],
        out_specs=vmem,
        scratch_shapes=scratch,
        compiler_params=pltpu.CompilerParams(
            collective_id=0,
            has_side_effects=True,
            vmem_limit_bytes=planned + 16 * 2**20,
        ),
        name="solve_and_route",
    )(rhs, couple_prev, diag_inverse, coupling, pair_block, pair_tile, pair_count, owner_slot)
    change = jnp.dot(rows_w, surface_factor, preferred_element_type=F32)
    return (schur.astype(F32) - change).astype(BF16)


def solution(mesh):
    placed = (
        P("col", "row"),
        P("row", None),
        P("row", None),
        P(("row", "col"), None, None),
        P(("row", "col")),
        P(("row", "col")),
        P(("row", "col")),
        P("row", None),
        P("row", "col"),
        P(None, "col"),
    )
    return jax.shard_map(
        functools.partial(shards, mesh.shape["row"], mesh.shape["col"]),
        mesh=mesh,
        in_specs=placed,
        out_specs=P("row", "col"),
        check_vma=False,
    )
```

```python
import functools

import jax
import jax.numpy as jnp
from jax import lax
from jax.experimental import pallas as pl
from jax.experimental.pallas import tpu as pltpu
from jax.sharding import PartitionSpec as P

CAP = 3
F32 = jnp.float32
BF16 = jnp.bfloat16
NT = (((1,), (1,)), ((), ()))


def dot(left, right):
    return jnp.dot(left, right, preferred_element_type=F32)


def halves(value):
    high = value.astype(BF16)
    return high, (value - high.astype(F32)).astype(BF16)


def kernel(
    n_rows,
    n_cols,
    rhs_hbm,
    couple_hbm,
    inverse_hbm,
    coupling_hbm,
    block_hbm,
    tile_hbm,
    count_hbm,
    slot_hbm,
    out,
    rhs,
    couple,
    inverse,
    coupling,
    block_ref,
    tile_ref,
    count_ref,
    slot_ref,
    couple_hi,
    inverse_hi,
    inverse_lo,
    chunks,
    gathered,
    dense,
    order,
    solved,
    before,
    right,
    partial,
    arrived,
    turned,
    load_sem,
    swap_send,
    swap_recv,
    share_send,
    share_recv,
    hop_sem,
    part_send,
    part_recv,
    turn_send,
    turn_recv,
):
    my_row = lax.axis_index("row")
    my_col = lax.axis_index("col")
    cols, width = rhs.shape
    held, tile, blk = coupling.shape
    per_row = width // blk
    tpr = slot_ref.shape[1]
    tpd = tpr // n_cols
    group = tpr * tile

    pairs = [
        (block_hbm, block_ref),
        (tile_hbm, tile_ref),
        (count_hbm, count_ref),
        (coupling_hbm, coupling),
        (inverse_hbm, inverse),
        (rhs_hbm, rhs),
        (couple_hbm, couple),
        (slot_hbm, slot_ref),
    ]
    loads = [
        pltpu.make_async_copy(source, target, load_sem.at[i])
        for i, (source, target) in enumerate(pairs)
    ]
    for load in loads:
        load.start()

    def row_peer(step):
        return {"row": lax.rem(my_row + step, n_rows)}

    def col_peer(step):
        return {"col": lax.rem(my_col + step, n_cols)}

    pair = 2 if n_cols % 2 == 0 else 1
    line = n_cols // pair

    def pair_up(send, recv, block):
        lane = lax.rem(my_col, pair)
        major = my_col // pair
        near, far = [], []

        def push(index, target, number):
            return pltpu.make_async_remote_copy(
                src_ref=block(index),
                dst_ref=block(index),
                send_sem=send.at[number],
                recv_sem=recv.at[number],
                device_id={"col": target},
                device_id_type=pl.DeviceIdType.MESH,
            )

        for step in range(1, line):
            near.append(push(my_col, lax.rem(major + step, line) * pair + lane, step))
        for step in range(line):
            source = lax.rem(major + line - step, line) * pair + lane
            if pair > 1:
                far.append(push(source, major * pair + 1 - lane, line + step))
        return near, far

    def forward(near, far):
        for step in range(1, line):
            near[step - 1].wait_recv()
            for copy in far[step : step + 1]:
                copy.start()

    barrier = pltpu.get_barrier_semaphore()
    for step in range(1, n_rows):
        pl.semaphore_signal(
            barrier, inc=1, device_id=row_peer(step), device_id_type=pl.DeviceIdType.MESH
        )
    for step in range(1, n_cols):
        pl.semaphore_signal(
            barrier, inc=1, device_id=col_peer(step), device_id_type=pl.DeviceIdType.MESH
        )

    for load in loads[:4]:
        load.wait()

    count = count_ref[0]
    keys, codes = [], []
    sources = []
    for k in range(held):
        block = block_ref[k]
        source = lax.div(block, per_row)
        rank = jnp.int32(0)
        for j in range(k):
            rank = rank + jnp.where(sources[j] == source, 1, 0)
        sources.append(jnp.where(k < count, source, -1))
        keys.append(jnp.where(k < count, source * CAP + rank, -1))
        codes.append(tile_ref[k] * per_row + block - source * per_row)
    lines = lax.broadcasted_iota(jnp.int32, (tile, blk), 0)
    for r in range(n_rows):
        marks = jnp.full((tile, blk), -1, jnp.int32)
        for s in range(CAP):
            place, code = jnp.int32(0), jnp.int32(-1)
            for k in range(held):
                hit = keys[k] == r * CAP + s
                place = jnp.where(hit, k, place)
                code = jnp.where(hit, codes[k], code)
            chunks[r, s * tile : (s + 1) * tile, :] = coupling[place]
            marks = jnp.where(lines == s, code, marks)
        chunks[r, CAP * tile : (CAP + 1) * tile, :] = marks.astype(F32).astype(BF16)
    gathered[my_col, my_row] = chunks[my_row]

    pl.semaphore_wait(barrier, n_rows + n_cols - 2)

    swaps = []
    for step in range(1, n_rows):
        swap = pltpu.make_async_remote_copy(
            src_ref=chunks.at[lax.rem(my_row + step, n_rows)],
            dst_ref=gathered.at[my_col, my_row],
            send_sem=swap_send.at[step],
            recv_sem=swap_recv.at[step],
            device_id=row_peer(step),
            device_id_type=pl.DeviceIdType.MESH,
        )
        swap.start()
        swaps.append(swap)

    loads[4].wait()
    loads[5].wait()
    high, low = halves(inverse[...])
    inverse_hi[...] = high
    inverse_lo[...] = low
    loads[6].wait()
    loads[7].wait()

    @pl.when(my_row > 0)
    def _():
        couple_hi[...] = couple[...].astype(BF16)

    for swap in swaps:
        swap.wait()
    near, far = pair_up(share_send, share_recv, lambda index: gathered.at[index])
    for copy in far[:1] + near:
        copy.start()

    hop = pltpu.make_async_remote_copy(
        src_ref=solved,
        dst_ref=before,
        send_sem=hop_sem.at[0],
        recv_sem=hop_sem.at[1],
        device_id=row_peer(1),
        device_id_type=pl.DeviceIdType.MESH,
    )

    def chain():
        right[...] = rhs[...]

        @pl.when(my_row > 0)
        def _():
            hop.wait_recv()
            known = before[...]
            right[...] = rhs[...] - dot(known, couple_hi[...])

        high, low = halves(right[...])
        both = dot(jnp.concatenate([high, low], axis=0), inverse_hi[...])
        solved[...] = (both[:cols] + both[cols:] + dot(high, inverse_lo[...])).astype(BF16)

    half = n_rows // 2

    @pl.when(my_row < half)
    def _():
        chain()
        hop.start()

    forward(near, far)

    @pl.when((my_row >= half) & (my_row < n_rows - 1))
    def _():
        chain()
        hop.start()

    for copy in far:
        copy.wait_recv()

    def spread(index, _):
        c = index // n_rows
        r = index % n_rows
        marks = gathered[c, r, CAP * tile : (CAP + 1) * tile, :].astype(F32)
        tiles = [gathered[c, r, s * tile : (s + 1) * tile, :] for s in range(CAP)]
        where = [
            jnp.broadcast_to(marks[s : s + 1, :], (tile, blk)).astype(BF16) for s in range(CAP)
        ]
        base = (r * n_cols + c) * (tpd * tile)
        zero = jnp.zeros((tile, blk), BF16)
        for t in range(tpd):
            for j in range(per_row):
                total = zero
                for s in range(CAP):
                    total = total + jnp.where(where[s] == t * per_row + j, tiles[s], zero)
                dense[
                    pl.ds(pl.multiple_of(base + t * tile, tile), tile), j * blk : (j + 1) * blk
                ] = total
        return 0

    lax.fori_loop(0, n_rows * n_cols, spread, 0)

    ahead = lax.broadcasted_iota(jnp.int32, (tile, group), 1)
    down = lax.broadcasted_iota(jnp.int32, (tile, group), 0)
    for i in range(tpr):
        same = ahead == slot_ref[0, i] * tile + down
        order[i * tile : (i + 1) * tile, :] = jnp.where(same, 1.0, 0.0).astype(BF16)

    @pl.when(my_row == n_rows - 1)
    def _():
        chain()

    def product(r):
        rows = pl.ds(pl.multiple_of(r * group, group), group)
        return lax.dot_general(solved[...], dense[rows, :], NT, preferred_element_type=F32)

    parts = []
    for step in range(1, n_rows):
        partial[step] = product(lax.rem(my_row + step, n_rows)).astype(BF16)
        part = pltpu.make_async_remote_copy(
            src_ref=partial.at[step],
            dst_ref=arrived.at[step],
            send_sem=part_send.at[step],
            recv_sem=part_recv.at[step],
            device_id=row_peer(step),
            device_id_type=pl.DeviceIdType.MESH,
        )
        part.start()
        parts.append(part)
    total = product(my_row)
    for step in range(1, n_rows):
        parts[step - 1].wait_recv()
        total = total + arrived[step].astype(F32)
    mine = pl.ds(pl.multiple_of(my_col * cols, cols), cols)
    turned[mine, :] = total.astype(BF16)

    turn_near, turn_far = pair_up(
        turn_send,
        turn_recv,
        lambda index: turned.at[pl.ds(pl.multiple_of(index * cols, cols), cols)],
    )
    for copy in turn_far[:1] + turn_near:
        copy.start()
    forward(turn_near, turn_far)
    for copy in turn_far:
        copy.wait_recv()
    out[...] = lax.dot_general(
        order[...], turned[...], NT, preferred_element_type=F32
    ).astype(BF16)

    for copy in near + far + parts + turn_near + turn_far:
        copy.wait_send()

    @pl.when(my_row < n_rows - 1)
    def _():
        hop.wait_send()


def shards(
    n_rows,
    n_cols,
    rhs,
    couple_prev,
    diag_inverse,
    coupling,
    pair_block,
    pair_tile,
    pair_count,
    owner_slot,
    schur,
    surface_factor,
):
    cols, width = rhs.shape
    held, tile, blk = coupling.shape
    group = owner_slot.shape[1] * tile
    chunk = (CAP + 1) * tile
    dma = pltpu.SemaphoreType.DMA
    vmem = pl.BlockSpec(memory_space=pltpu.VMEM)
    hbm = pl.BlockSpec(memory_space=pltpu.HBM)
    scratch = [
        pltpu.VMEM((cols, width), F32),
        pltpu.VMEM((width, width), F32),
        pltpu.VMEM((width, width), F32),
        pltpu.VMEM((held, tile, blk), BF16),
        pltpu.SMEM((held,), jnp.int32),
        pltpu.SMEM((held,), jnp.int32),
        pltpu.SMEM((1,), jnp.int32),
        pltpu.SMEM(owner_slot.shape, jnp.int32),
        pltpu.VMEM((width, width), BF16),
        pltpu.VMEM((width, width), BF16),
        pltpu.VMEM((width, width), BF16),
        pltpu.VMEM((n_rows, chunk, blk), BF16),
        pltpu.VMEM((n_cols, n_rows, chunk, blk), BF16),
        pltpu.VMEM((n_rows * group, width), BF16),
        pltpu.VMEM((group, group), BF16),
        pltpu.VMEM((cols, width), BF16),
        pltpu.VMEM((cols, width), BF16),
        pltpu.VMEM((cols, width), F32),
        pltpu.VMEM((n_rows, cols, group), BF16),
        pltpu.VMEM((n_rows, cols, group), BF16),
        pltpu.VMEM((n_cols * cols, group), BF16),
        dma((8,)),
        dma((n_rows,)),
        dma((n_rows,)),
        dma((n_cols + 1,)),
        dma((n_cols + 1,)),
        dma((2,)),
        dma((n_rows,)),
        dma((n_rows,)),
        dma((n_cols + 1,)),
        dma((n_cols + 1,)),
    ]
    rows_w = pl.pallas_call(
        functools.partial(kernel, n_rows, n_cols),
        out_shape=jax.ShapeDtypeStruct((group, n_cols * cols), BF16),
        in_specs=[hbm] * 8,
        out_specs=vmem,
        scratch_shapes=scratch,
        compiler_params=pltpu.CompilerParams(
            collective_id=0,
            has_side_effects=True,
            vmem_limit_bytes=64 * 2**20 - 2**16,
        ),
        name="solve_and_route",
    )(rhs, couple_prev, diag_inverse, coupling, pair_block, pair_tile, pair_count, owner_slot)
    change = jnp.dot(rows_w, surface_factor, preferred_element_type=F32)
    return (schur.astype(F32) - change).astype(BF16)


def solution(mesh):
    placed = (
        P("col", "row"),
        P("row", None),
        P("row", None),
        P(("row", "col"), None, None),
        P(("row", "col")),
        P(("row", "col")),
        P(("row", "col")),
        P("row", None),
        P("row", "col"),
        P(None, "col"),
    )
    return jax.shard_map(
        functools.partial(shards, mesh.shape["row"], mesh.shape["col"]),
        mesh=mesh,
        in_specs=placed,
        out_specs=P("row", "col"),
        check_vma=False,
    )
```

```python
import functools

import jax
import jax.numpy as jnp
from jax import lax
from jax.experimental import pallas as pl
from jax.experimental.pallas import tpu as pltpu
from jax.sharding import PartitionSpec as P

CAP = 3
HOPS = 4
VMEM = 64 * 2**20 - 2**16
F32 = jnp.float32
BF16 = jnp.bfloat16
NT = (((1,), (1,)), ((), ()))


def dot(left, right):
    return jnp.dot(left, right, preferred_element_type=F32)


def halves(value):
    high = value.astype(BF16)
    return high, (value - high.astype(F32)).astype(BF16)


def kernel(
    n_rows,
    n_cols,
    rhs_hbm,
    couple_hbm,
    inverse_hbm,
    coupling_hbm,
    block_hbm,
    tile_hbm,
    count_hbm,
    slot_hbm,
    out,
    rhs,
    couple,
    inverse,
    coupling,
    block_ref,
    tile_ref,
    count_ref,
    slot_ref,
    couple_hi,
    inverse_hi,
    inverse_lo,
    chunks,
    gathered,
    dense,
    order,
    solved,
    before,
    partial,
    arrived,
    turned,
    load_sem,
    swap_send,
    swap_recv,
    share_send,
    share_recv,
    hop_send,
    hop_recv,
    part_send,
    part_recv,
    turn_send,
    turn_recv,
):
    my_row = lax.axis_index("row")
    my_col = lax.axis_index("col")
    cols, width = rhs.shape
    held, tile, blk = coupling.shape
    per_row = width // blk
    tpr = slot_ref.shape[1]
    tpd = tpr // n_cols
    group = tpr * tile

    pairs = [
        (block_hbm, block_ref),
        (tile_hbm, tile_ref),
        (count_hbm, count_ref),
        (coupling_hbm, coupling),
        (inverse_hbm, inverse),
        (rhs_hbm, rhs),
        (couple_hbm, couple),
        (slot_hbm, slot_ref),
    ]
    loads = [
        pltpu.make_async_copy(source, target, load_sem.at[i])
        for i, (source, target) in enumerate(pairs)
    ]
    for load in loads:
        load.start()

    def row_peer(step):
        return {"row": lax.rem(my_row + step, n_rows)}

    def col_peer(step):
        return {"col": lax.rem(my_col + step, n_cols)}

    pair = 2 if n_cols % 2 == 0 else 1
    line = n_cols // pair

    def pair_up(send, recv, block):
        lane = lax.rem(my_col, pair)
        major = my_col // pair
        near, far = [], []

        def push(index, target, number):
            return pltpu.make_async_remote_copy(
                src_ref=block(index),
                dst_ref=block(index),
                send_sem=send.at[number],
                recv_sem=recv.at[number],
                device_id={"col": target},
                device_id_type=pl.DeviceIdType.MESH,
            )

        for step in range(1, line):
            near.append(push(my_col, lax.rem(major + step, line) * pair + lane, step))
        for step in range(line):
            source = lax.rem(major + line - step, line) * pair + lane
            if pair > 1:
                far.append(push(source, major * pair + 1 - lane, line + step))
        return near, far

    def forward(near, far):
        for step in range(1, line):
            near[step - 1].wait_recv()
            for copy in far[step : step + 1]:
                copy.start()

    barrier = pltpu.get_barrier_semaphore()
    for step in range(1, n_rows):
        pl.semaphore_signal(
            barrier, inc=1, device_id=row_peer(step), device_id_type=pl.DeviceIdType.MESH
        )
    for step in range(1, n_cols):
        pl.semaphore_signal(
            barrier, inc=1, device_id=col_peer(step), device_id_type=pl.DeviceIdType.MESH
        )

    for load in loads[:4]:
        load.wait()

    count = count_ref[0]
    keys, codes = [], []
    sources = []
    for k in range(held):
        block = block_ref[k]
        source = lax.div(block, per_row)
        rank = jnp.int32(0)
        for j in range(k):
            rank = rank + jnp.where(sources[j] == source, 1, 0)
        sources.append(jnp.where(k < count, source, -1))
        keys.append(jnp.where(k < count, source * CAP + rank, -1))
        codes.append(tile_ref[k] * per_row + block - source * per_row)
    lines = lax.broadcasted_iota(jnp.int32, (tile, blk), 0)
    for r in range(n_rows):
        marks = jnp.full((tile, blk), -1, jnp.int32)
        for s in range(CAP):
            place, code = jnp.int32(0), jnp.int32(-1)
            for k in range(held):
                hit = keys[k] == r * CAP + s
                place = jnp.where(hit, k, place)
                code = jnp.where(hit, codes[k], code)
            chunks[r, s * tile : (s + 1) * tile, :] = coupling[place]
            marks = jnp.where(lines == s, code, marks)
        chunks[r, CAP * tile : (CAP + 1) * tile, :] = marks.astype(F32).astype(BF16)
    gathered[my_col, my_row] = chunks[my_row]

    pl.semaphore_wait(barrier, n_rows + n_cols - 2)

    swaps = []
    for step in range(1, n_rows):
        swap = pltpu.make_async_remote_copy(
            src_ref=chunks.at[lax.rem(my_row + step, n_rows)],
            dst_ref=gathered.at[my_col, my_row],
            send_sem=swap_send.at[step],
            recv_sem=swap_recv.at[step],
            device_id=row_peer(step),
            device_id_type=pl.DeviceIdType.MESH,
        )
        swap.start()
        swaps.append(swap)

    loads[4].wait()
    loads[5].wait()
    high, low = halves(inverse[...])
    inverse_hi[...] = high
    inverse_lo[...] = low
    span = width // HOPS
    hops = []
    for h in range(HOPS):
        ahead = slice(h * span, (h + 1) * span)
        hops.append(
            pltpu.make_async_remote_copy(
                src_ref=solved.at[:, ahead],
                dst_ref=before.at[:, ahead],
                send_sem=hop_send.at[h],
                recv_sem=hop_recv.at[h],
                device_id=row_peer(1),
                device_id_type=pl.DeviceIdType.MESH,
            )
        )

    def chain(first, last):
        value = rhs[...]
        if not first:
            for h in range(HOPS):
                part = slice(h * span, (h + 1) * span)
                hops[h].wait_recv()
                value = value - dot(before[:, part], couple_hi[part, :])
        high, low = halves(value)
        stack = jnp.concatenate([high, low], axis=0)
        for h in range(HOPS):
            part = slice(h * span, (h + 1) * span)
            both = dot(stack, inverse_hi[:, part])
            solved[:, part] = (
                both[:cols] + both[cols:] + dot(high, inverse_lo[:, part])
            ).astype(BF16)
            if not last:
                hops[h].start()

    @pl.when(my_row == 0)
    def _():
        chain(True, n_rows == 1)

    loads[6].wait()
    loads[7].wait()

    @pl.when(my_row > 0)
    def _():
        couple_hi[...] = couple[...].astype(BF16)

    for swap in swaps:
        swap.wait()
    near, far = pair_up(share_send, share_recv, lambda index: gathered.at[index])
    for copy in far[:1] + near:
        copy.start()

    half = n_rows // 2

    @pl.when((my_row > 0) & (my_row < half))
    def _():
        chain(False, False)

    forward(near, far)

    @pl.when((my_row > 0) & (my_row >= half) & (my_row < n_rows - 1))
    def _():
        chain(False, False)

    for copy in far:
        copy.wait_recv()

    def spread(index, _):
        c = index // n_rows
        r = index % n_rows
        marks = gathered[c, r, CAP * tile : (CAP + 1) * tile, :].astype(F32)
        tiles = [gathered[c, r, s * tile : (s + 1) * tile, :] for s in range(CAP)]
        where = [
            jnp.broadcast_to(marks[s : s + 1, :], (tile, blk)).astype(BF16) for s in range(CAP)
        ]
        base = (r * n_cols + c) * (tpd * tile)
        zero = jnp.zeros((tile, blk), BF16)
        for t in range(tpd):
            for j in range(per_row):
                total = zero
                for s in range(CAP):
                    total = total + jnp.where(where[s] == t * per_row + j, tiles[s], zero)
                dense[
                    pl.ds(pl.multiple_of(base + t * tile, tile), tile), j * blk : (j + 1) * blk
                ] = total
        return 0

    lax.fori_loop(0, n_rows * n_cols, spread, 0)

    ahead = lax.broadcasted_iota(jnp.int32, (tile, group), 1)
    down = lax.broadcasted_iota(jnp.int32, (tile, group), 0)
    for i in range(tpr):
        same = ahead == slot_ref[0, i] * tile + down
        order[i * tile : (i + 1) * tile, :] = jnp.where(same, 1.0, 0.0).astype(BF16)

    @pl.when((my_row > 0) & (my_row == n_rows - 1))
    def _():
        chain(False, True)

    def product(r):
        rows = pl.ds(pl.multiple_of(r * group, group), group)
        return lax.dot_general(solved[...], dense[rows, :], NT, preferred_element_type=F32)

    parts = []
    for step in range(1, n_rows):
        partial[step] = product(lax.rem(my_row + step, n_rows)).astype(BF16)
        part = pltpu.make_async_remote_copy(
            src_ref=partial.at[step],
            dst_ref=arrived.at[step],
            send_sem=part_send.at[step],
            recv_sem=part_recv.at[step],
            device_id=row_peer(step),
            device_id_type=pl.DeviceIdType.MESH,
        )
        part.start()
        parts.append(part)
    total = product(my_row)
    for step in range(1, n_rows):
        parts[step - 1].wait_recv()
        total = total + arrived[step].astype(F32)
    mine = pl.ds(pl.multiple_of(my_col * cols, cols), cols)
    turned[mine, :] = total.astype(BF16)

    turn_near, turn_far = pair_up(
        turn_send,
        turn_recv,
        lambda index: turned.at[pl.ds(pl.multiple_of(index * cols, cols), cols)],
    )
    for copy in turn_far[:1] + turn_near:
        copy.start()
    forward(turn_near, turn_far)
    for copy in turn_far:
        copy.wait_recv()
    out[...] = lax.dot_general(
        order[...], turned[...], NT, preferred_element_type=F32
    ).astype(BF16)

    for copy in near + far + parts + turn_near + turn_far:
        copy.wait_send()

    @pl.when(my_row < n_rows - 1)
    def _():
        for hop in hops:
            hop.wait_send()


def update(rows_w, factor, schur, out):
    out[...] = (schur[...].astype(F32) - dot(rows_w[...], factor[...])).astype(BF16)


def shards(
    n_rows,
    n_cols,
    rhs,
    couple_prev,
    diag_inverse,
    coupling,
    pair_block,
    pair_tile,
    pair_count,
    owner_slot,
    schur,
    surface_factor,
):
    cols, width = rhs.shape
    held, tile, blk = coupling.shape
    group = owner_slot.shape[1] * tile
    chunk = (CAP + 1) * tile
    dma = pltpu.SemaphoreType.DMA
    vmem = pl.BlockSpec(memory_space=pltpu.VMEM)
    hbm = pl.BlockSpec(memory_space=pltpu.HBM)
    scratch = [
        pltpu.VMEM((cols, width), F32),
        pltpu.VMEM((width, width), F32),
        pltpu.VMEM((width, width), F32),
        pltpu.VMEM((held, tile, blk), BF16),
        pltpu.SMEM((held,), jnp.int32),
        pltpu.SMEM((held,), jnp.int32),
        pltpu.SMEM((1,), jnp.int32),
        pltpu.SMEM(owner_slot.shape, jnp.int32),
        pltpu.VMEM((width, width), BF16),
        pltpu.VMEM((width, width), BF16),
        pltpu.VMEM((width, width), BF16),
        pltpu.VMEM((n_rows, chunk, blk), BF16),
        pltpu.VMEM((n_cols, n_rows, chunk, blk), BF16),
        pltpu.VMEM((n_rows * group, width), BF16),
        pltpu.VMEM((group, group), BF16),
        pltpu.VMEM((cols, width), BF16),
        pltpu.VMEM((cols, width), BF16),
        pltpu.VMEM((n_rows, cols, group), BF16),
        pltpu.VMEM((n_rows, cols, group), BF16),
        pltpu.VMEM((n_cols * cols, group), BF16),
        dma((8,)),
        dma((n_rows,)),
        dma((n_rows,)),
        dma((n_cols + 1,)),
        dma((n_cols + 1,)),
        dma((HOPS,)),
        dma((HOPS,)),
        dma((n_rows,)),
        dma((n_rows,)),
        dma((n_cols + 1,)),
        dma((n_cols + 1,)),
    ]
    rows_w = pl.pallas_call(
        functools.partial(kernel, n_rows, n_cols),
        out_shape=jax.ShapeDtypeStruct((group, n_cols * cols), BF16),
        in_specs=[hbm] * 8,
        out_specs=vmem,
        scratch_shapes=scratch,
        compiler_params=pltpu.CompilerParams(
            collective_id=0,
            has_side_effects=True,
            vmem_limit_bytes=VMEM,
        ),
        name="solve_and_route",
    )(rhs, couple_prev, diag_inverse, coupling, pair_block, pair_tile, pair_count, owner_slot)
    rows, columns = schur.shape
    depth = surface_factor.shape[0]
    step = 4 * blk if columns % (4 * blk) == 0 else blk
    return pl.pallas_call(
        update,
        out_shape=jax.ShapeDtypeStruct((rows, columns), BF16),
        grid=(columns // step,),
        in_specs=[
            pl.BlockSpec((rows, depth), lambda i: (0, 0)),
            pl.BlockSpec((depth, step), lambda i: (0, i)),
            pl.BlockSpec((rows, step), lambda i: (0, i)),
        ],
        out_specs=pl.BlockSpec((rows, step), lambda i: (0, i)),
        compiler_params=pltpu.CompilerParams(vmem_limit_bytes=VMEM),
        name="slab_update",
    )(rows_w, surface_factor, schur)


def solution(mesh):
    placed = (
        P("col", "row"),
        P("row", None),
        P("row", None),
        P(("row", "col"), None, None),
        P(("row", "col")),
        P(("row", "col")),
        P(("row", "col")),
        P("row", None),
        P("row", "col"),
        P(None, "col"),
    )
    return jax.shard_map(
        functools.partial(shards, mesh.shape["row"], mesh.shape["col"]),
        mesh=mesh,
        in_specs=placed,
        out_specs=P("row", "col"),
        check_vma=False,
    )
```

```python
import functools

import jax
import jax.numpy as jnp
from jax import lax
from jax.experimental import pallas as pl
from jax.experimental.pallas import tpu as pltpu
from jax.sharding import PartitionSpec as P

CAP = 3
HOPS = 4
VMEM = 64 * 2**20
F32 = jnp.float32
BF16 = jnp.bfloat16
NT = (((1,), (1,)), ((), ()))


def dot(left, right):
    return jnp.dot(left, right, preferred_element_type=F32)


def halves(value):
    high = value.astype(BF16)
    return high, (value - high.astype(F32)).astype(BF16)


def kernel(
    n_rows,
    n_cols,
    rhs_hbm,
    couple_hbm,
    inverse_hbm,
    coupling_hbm,
    block_hbm,
    tile_hbm,
    count_hbm,
    slot_hbm,
    out,
    rhs,
    couple,
    inverse,
    coupling,
    block_ref,
    tile_ref,
    count_ref,
    slot_ref,
    couple_hi,
    inverse_hi,
    inverse_lo,
    chunks,
    gathered,
    dense,
    order,
    solved,
    before,
    partial,
    arrived,
    turned,
    load_sem,
    swap_send,
    swap_recv,
    share_send,
    share_recv,
    hop_send,
    hop_recv,
    part_send,
    part_recv,
    turn_send,
    turn_recv,
):
    my_row = lax.axis_index("row")
    my_col = lax.axis_index("col")
    cols, width = rhs.shape
    held, tile, blk = coupling.shape
    per_row = width // blk
    tpr = slot_ref.shape[1]
    tpd = tpr // n_cols
    group = tpr * tile

    pairs = [
        (block_hbm, block_ref),
        (tile_hbm, tile_ref),
        (count_hbm, count_ref),
        (coupling_hbm, coupling),
        (inverse_hbm, inverse),
        (rhs_hbm, rhs),
        (couple_hbm, couple),
        (slot_hbm, slot_ref),
    ]
    loads = [
        pltpu.make_async_copy(source, target, load_sem.at[i])
        for i, (source, target) in enumerate(pairs)
    ]
    for load in loads:
        load.start()

    def row_peer(step):
        return {"row": lax.rem(my_row + step, n_rows)}

    def col_peer(step):
        return {"col": lax.rem(my_col + step, n_cols)}

    pair = 2 if n_cols % 2 == 0 else 1
    line = n_cols // pair

    def pair_up(send, recv, block):
        lane = lax.rem(my_col, pair)
        major = my_col // pair
        near, far = [], []

        def push(index, target, number):
            return pltpu.make_async_remote_copy(
                src_ref=block(index),
                dst_ref=block(index),
                send_sem=send.at[number],
                recv_sem=recv.at[number],
                device_id={"col": target},
                device_id_type=pl.DeviceIdType.MESH,
            )

        for step in range(1, line):
            near.append(push(my_col, lax.rem(major + step, line) * pair + lane, step))
        for step in range(line):
            source = lax.rem(major + line - step, line) * pair + lane
            if pair > 1:
                far.append(push(source, major * pair + 1 - lane, line + step))
        return near, far

    def forward(near, far):
        for step in range(1, line):
            near[step - 1].wait_recv()
            for copy in far[step : step + 1]:
                copy.start()

    barrier = pltpu.get_barrier_semaphore()
    for step in range(1, n_rows):
        pl.semaphore_signal(
            barrier, inc=1, device_id=row_peer(step), device_id_type=pl.DeviceIdType.MESH
        )
    for step in range(1, n_cols):
        pl.semaphore_signal(
            barrier, inc=1, device_id=col_peer(step), device_id_type=pl.DeviceIdType.MESH
        )

    for load in loads[:4]:
        load.wait()

    count = count_ref[0]
    keys, codes = [], []
    sources = []
    for k in range(held):
        block = block_ref[k]
        source = lax.div(block, per_row)
        rank = jnp.int32(0)
        for j in range(k):
            rank = rank + jnp.where(sources[j] == source, 1, 0)
        sources.append(jnp.where(k < count, source, -1))
        keys.append(jnp.where(k < count, source * CAP + rank, -1))
        codes.append(tile_ref[k] * per_row + block - source * per_row)
    lines = lax.broadcasted_iota(jnp.int32, (tile, blk), 0)
    for r in range(n_rows):
        marks = jnp.full((tile, blk), -1, jnp.int32)
        for s in range(CAP):
            place, code = jnp.int32(0), jnp.int32(-1)
            for k in range(held):
                hit = keys[k] == r * CAP + s
                place = jnp.where(hit, k, place)
                code = jnp.where(hit, codes[k], code)
            chunks[r, s * tile : (s + 1) * tile, :] = coupling[place]
            marks = jnp.where(lines == s, code, marks)
        chunks[r, CAP * tile : (CAP + 1) * tile, :] = marks.astype(F32).astype(BF16)
    gathered[my_col, my_row] = chunks[my_row]

    pl.semaphore_wait(barrier, n_rows + n_cols - 2)

    swaps = []
    for step in range(1, n_rows):
        swap = pltpu.make_async_remote_copy(
            src_ref=chunks.at[lax.rem(my_row + step, n_rows)],
            dst_ref=gathered.at[my_col, my_row],
            send_sem=swap_send.at[step],
            recv_sem=swap_recv.at[step],
            device_id=row_peer(step),
            device_id_type=pl.DeviceIdType.MESH,
        )
        swap.start()
        swaps.append(swap)

    span = width // HOPS
    hops = []
    for h in range(HOPS):
        ahead = slice(h * span, (h + 1) * span)
        hops.append(
            pltpu.make_async_remote_copy(
                src_ref=solved.at[:, ahead],
                dst_ref=before.at[:, ahead],
                send_sem=hop_send.at[h],
                recv_sem=hop_recv.at[h],
                device_id=row_peer(1),
                device_id_type=pl.DeviceIdType.MESH,
            )
        )

    def chain(first, last):
        value = rhs[...]
        if not first:
            for h in range(HOPS):
                part = slice(h * span, (h + 1) * span)
                hops[h].wait_recv()
                value = value - dot(before[:, part], couple_hi[part, :])
        high, low = halves(value)
        stack = jnp.concatenate([high, low], axis=0)
        for h in range(HOPS):
            part = slice(h * span, (h + 1) * span)
            both = dot(stack, inverse_hi[:, part])
            solved[:, part] = (
                both[:cols] + both[cols:] + dot(high, inverse_lo[:, part])
            ).astype(BF16)
            if not last:
                hops[h].start()

    def split():
        high, low = halves(inverse[...])
        inverse_hi[...] = high
        inverse_lo[...] = low

    loads[4].wait()
    loads[5].wait()

    @pl.when(my_row == 0)
    def _():
        split()
        chain(True, n_rows == 1)

    for swap in swaps:
        swap.wait()
    near, far = pair_up(share_send, share_recv, lambda index: gathered.at[index])
    for copy in far[:1] + near:
        copy.start()

    loads[6].wait()
    loads[7].wait()

    @pl.when(my_row > 0)
    def _():
        split()
        couple_hi[...] = couple[...].astype(BF16)

    half = n_rows // 2

    @pl.when((my_row > 0) & (my_row < half))
    def _():
        chain(False, False)

    forward(near, far)

    @pl.when((my_row > 0) & (my_row >= half) & (my_row < n_rows - 1))
    def _():
        chain(False, False)

    for copy in far:
        copy.wait_recv()

    def spread(index, _):
        c = index // n_rows
        r = index % n_rows
        marks = gathered[c, r, CAP * tile : (CAP + 1) * tile, :].astype(F32)
        tiles = [gathered[c, r, s * tile : (s + 1) * tile, :] for s in range(CAP)]
        rows = [jnp.broadcast_to(marks[s : s + 1, :], (tile, blk)) for s in range(CAP)]
        base = (r * n_cols + c) * (tpd * tile)

        def gate(test):
            return jnp.where(test, 1.0, 0.0).astype(BF16)

        gates = []
        kept = []
        for s in range(CAP):
            least = [rows[s] >= float(t * per_row) for t in range(tpd + 1)]
            kept.append(
                [tiles[s] * gate(least[t] & ~least[t + 1]) for t in range(tpd)]
            )
            local = rows[s]
            for t in range(1, tpd):
                local = local - jnp.where(least[t], float(per_row), 0.0)
            gates.append([gate(local == float(j)) for j in range(per_row)])
        for t in range(tpd):
            for j in range(per_row):
                total = kept[0][t] * gates[0][j]
                for s in range(1, CAP):
                    total = total + kept[s][t] * gates[s][j]
                dense[
                    pl.ds(pl.multiple_of(base + t * tile, tile), tile), j * blk : (j + 1) * blk
                ] = total
        return 0

    lax.fori_loop(0, n_rows * n_cols, spread, 0)

    ahead = lax.broadcasted_iota(jnp.int32, (tile, group), 1)
    down = lax.broadcasted_iota(jnp.int32, (tile, group), 0)
    for i in range(tpr):
        same = ahead == slot_ref[0, i] * tile + down
        order[i * tile : (i + 1) * tile, :] = jnp.where(same, 1.0, 0.0).astype(BF16)

    @pl.when((my_row > 0) & (my_row == n_rows - 1))
    def _():
        chain(False, True)

    def product(r):
        rows = pl.ds(pl.multiple_of(r * group, group), group)
        return lax.dot_general(dense[rows, :], solved[...], NT, preferred_element_type=F32).T

    parts = []
    for step in range(1, n_rows):
        partial[step] = product(lax.rem(my_row + step, n_rows)).astype(BF16)
        part = pltpu.make_async_remote_copy(
            src_ref=partial.at[step],
            dst_ref=arrived.at[step],
            send_sem=part_send.at[step],
            recv_sem=part_recv.at[step],
            device_id=row_peer(step),
            device_id_type=pl.DeviceIdType.MESH,
        )
        part.start()
        parts.append(part)
    total = product(my_row)
    for step in range(1, n_rows):
        parts[step - 1].wait_recv()
        total = total + arrived[step].astype(F32)
    mine = pl.ds(pl.multiple_of(my_col * cols, cols), cols)
    turned[mine, :] = total.astype(BF16)

    turn_near, turn_far = pair_up(
        turn_send,
        turn_recv,
        lambda index: turned.at[pl.ds(pl.multiple_of(index * cols, cols), cols)],
    )
    for copy in turn_far[:1] + turn_near:
        copy.start()
    forward(turn_near, turn_far)
    for copy in turn_far:
        copy.wait_recv()
    out[...] = lax.dot_general(
        order[...], turned[...], NT, preferred_element_type=F32
    ).astype(BF16)

    for copy in near + far + parts + turn_near + turn_far:
        copy.wait_send()

    @pl.when(my_row < n_rows - 1)
    def _():
        for hop in hops:
            hop.wait_send()


def shards(
    n_rows,
    n_cols,
    rhs,
    couple_prev,
    diag_inverse,
    coupling,
    pair_block,
    pair_tile,
    pair_count,
    owner_slot,
    schur,
    surface_factor,
):
    cols, width = rhs.shape
    held, tile, blk = coupling.shape
    group = owner_slot.shape[1] * tile
    chunk = (CAP + 1) * tile
    dma = pltpu.SemaphoreType.DMA
    vmem = pl.BlockSpec(memory_space=pltpu.VMEM)
    hbm = pl.BlockSpec(memory_space=pltpu.HBM)
    scratch = [
        pltpu.VMEM((cols, width), F32),
        pltpu.VMEM((width, width), F32),
        pltpu.VMEM((width, width), F32),
        pltpu.VMEM((held, tile, blk), BF16),
        pltpu.SMEM((held,), jnp.int32),
        pltpu.SMEM((held,), jnp.int32),
        pltpu.SMEM((1,), jnp.int32),
        pltpu.SMEM(owner_slot.shape, jnp.int32),
        pltpu.VMEM((width, width), BF16),
        pltpu.VMEM((width, width), BF16),
        pltpu.VMEM((width, width), BF16),
        pltpu.VMEM((n_rows, chunk, blk), BF16),
        pltpu.VMEM((n_cols, n_rows, chunk, blk), BF16),
        pltpu.VMEM((n_rows * group, width), BF16),
        pltpu.VMEM((group, group), BF16),
        pltpu.VMEM((cols, width), BF16),
        pltpu.VMEM((cols, width), BF16),
        pltpu.VMEM((n_rows, cols, group), BF16),
        pltpu.VMEM((n_rows, cols, group), BF16),
        pltpu.VMEM((n_cols * cols, group), BF16),
        dma((8,)),
        dma((n_rows,)),
        dma((n_rows,)),
        dma((n_cols + 1,)),
        dma((n_cols + 1,)),
        dma((HOPS,)),
        dma((HOPS,)),
        dma((n_rows,)),
        dma((n_rows,)),
        dma((n_cols + 1,)),
        dma((n_cols + 1,)),
    ]
    beside = 2 * (schur.size + surface_factor.size)
    rows_w = pl.pallas_call(
        functools.partial(kernel, n_rows, n_cols),
        out_shape=jax.ShapeDtypeStruct((group, n_cols * cols), BF16),
        in_specs=[hbm] * 8,
        out_specs=vmem,
        scratch_shapes=scratch,
        compiler_params=pltpu.CompilerParams(
            collective_id=0,
            has_side_effects=True,
            vmem_limit_bytes=VMEM - beside - 2**20,
        ),
        name="solve_and_route",
    )(rhs, couple_prev, diag_inverse, coupling, pair_block, pair_tile, pair_count, owner_slot)
    change = jnp.dot(rows_w, surface_factor, preferred_element_type=F32)
    return (schur.astype(F32) - change).astype(BF16)


def solution(mesh):
    placed = (
        P("col", "row"),
        P("row", None),
        P("row", None),
        P(("row", "col"), None, None),
        P(("row", "col")),
        P(("row", "col")),
        P(("row", "col")),
        P("row", None),
        P("row", "col"),
        P(None, "col"),
    )
    return jax.shard_map(
        functools.partial(shards, mesh.shape["row"], mesh.shape["col"]),
        mesh=mesh,
        in_specs=placed,
        out_specs=P("row", "col"),
        check_vma=False,
    )
```

```python
import functools

import jax
import jax.numpy as jnp
from jax import lax
from jax.experimental import pallas as pl
from jax.experimental.pallas import tpu as pltpu
from jax.sharding import PartitionSpec as P

CAP = 3
HOPS = 4
VMEM = 64 * 2**20
F32 = jnp.float32
BF16 = jnp.bfloat16
NT = (((1,), (1,)), ((), ()))


def dot(left, right):
    return jnp.dot(left, right, preferred_element_type=F32)


def halves(value):
    high = value.astype(BF16)
    return high, (value - high.astype(F32)).astype(BF16)


def kernel(
    n_rows,
    n_cols,
    rhs_hbm,
    couple_hbm,
    inverse_hbm,
    coupling_hbm,
    block_hbm,
    tile_hbm,
    count_hbm,
    slot_hbm,
    out,
    rhs,
    couple,
    inverse,
    coupling,
    block_ref,
    tile_ref,
    count_ref,
    slot_ref,
    couple_hi,
    inverse_hi,
    inverse_lo,
    chunks,
    gathered,
    dense,
    order,
    solved,
    before,
    partial,
    arrived,
    turned,
    load_sem,
    swap_send,
    swap_recv,
    share_send,
    share_recv,
    hop_send,
    hop_recv,
    part_send,
    part_recv,
    turn_send,
    turn_recv,
):
    my_row = lax.axis_index("row")
    my_col = lax.axis_index("col")
    cols, width = rhs.shape
    held, tile, blk = coupling.shape
    per_row = width // blk
    tpr = slot_ref.shape[1]
    tpd = tpr // n_cols
    group = tpr * tile

    pairs = [
        (block_hbm, block_ref),
        (tile_hbm, tile_ref),
        (count_hbm, count_ref),
        (coupling_hbm, coupling),
        (inverse_hbm, inverse),
        (rhs_hbm, rhs),
        (couple_hbm, couple),
        (slot_hbm, slot_ref),
    ]
    loads = [
        pltpu.make_async_copy(source, target, load_sem.at[i])
        for i, (source, target) in enumerate(pairs)
    ]
    for load in loads:
        load.start()

    def row_peer(step):
        return {"row": lax.rem(my_row + step, n_rows)}

    def col_peer(step):
        return {"col": lax.rem(my_col + step, n_cols)}

    pair = 2 if n_cols % 2 == 0 else 1
    line = n_cols // pair

    def pair_up(send, recv, block, base=0):
        lane = lax.rem(my_col, pair)
        major = my_col // pair
        near, far = [], []

        def push(index, target, number):
            return pltpu.make_async_remote_copy(
                src_ref=block(index),
                dst_ref=block(index),
                send_sem=send.at[base + number],
                recv_sem=recv.at[base + number],
                device_id={"col": target},
                device_id_type=pl.DeviceIdType.MESH,
            )

        for step in range(1, line):
            near.append(push(my_col, lax.rem(major + step, line) * pair + lane, step))
        for step in range(line):
            source = lax.rem(major + line - step, line) * pair + lane
            if pair > 1:
                far.append(push(source, major * pair + 1 - lane, line + step))
        return near, far

    def forward(near, far):
        for step in range(1, line):
            near[step - 1].wait_recv()
            for copy in far[step : step + 1]:
                copy.start()

    barrier = pltpu.get_barrier_semaphore()
    for step in range(1, n_rows):
        pl.semaphore_signal(
            barrier, inc=1, device_id=row_peer(step), device_id_type=pl.DeviceIdType.MESH
        )
    for step in range(1, n_cols):
        pl.semaphore_signal(
            barrier, inc=1, device_id=col_peer(step), device_id_type=pl.DeviceIdType.MESH
        )

    for load in loads[:4]:
        load.wait()

    count = count_ref[0]
    keys, codes = [], []
    sources = []
    for k in range(held):
        block = block_ref[k]
        source = lax.div(block, per_row)
        rank = jnp.int32(0)
        for j in range(k):
            rank = rank + jnp.where(sources[j] == source, 1, 0)
        sources.append(jnp.where(k < count, source, -1))
        keys.append(jnp.where(k < count, source * CAP + rank, -1))
        codes.append(tile_ref[k] * per_row + block - source * per_row)
    lines = lax.broadcasted_iota(jnp.int32, (tile, blk), 0)
    for r in range(n_rows):
        marks = jnp.full((tile, blk), -1, jnp.int32)
        for s in range(CAP):
            place, code = jnp.int32(0), jnp.int32(-1)
            for k in range(held):
                hit = keys[k] == r * CAP + s
                place = jnp.where(hit, k, place)
                code = jnp.where(hit, codes[k], code)
            chunks[r, s * tile : (s + 1) * tile, :] = coupling[place]
            marks = jnp.where(lines == s, code, marks)
        chunks[r, CAP * tile : (CAP + 1) * tile, :] = marks.astype(F32).astype(BF16)
    gathered[my_col, my_row] = chunks[my_row]

    pl.semaphore_wait(barrier, n_rows + n_cols - 2)

    swaps = []
    for step in range(1, n_rows):
        swap = pltpu.make_async_remote_copy(
            src_ref=chunks.at[lax.rem(my_row + step, n_rows)],
            dst_ref=gathered.at[my_col, my_row],
            send_sem=swap_send.at[step],
            recv_sem=swap_recv.at[step],
            device_id=row_peer(step),
            device_id_type=pl.DeviceIdType.MESH,
        )
        swap.start()
        swaps.append(swap)

    span = width // HOPS
    hops = []
    for h in range(HOPS):
        ahead = slice(h * span, (h + 1) * span)
        hops.append(
            pltpu.make_async_remote_copy(
                src_ref=solved.at[:, ahead],
                dst_ref=before.at[:, ahead],
                send_sem=hop_send.at[h],
                recv_sem=hop_recv.at[h],
                device_id=row_peer(1),
                device_id_type=pl.DeviceIdType.MESH,
            )
        )

    def chain(first, last):
        value = rhs[...]
        if not first:
            for h in range(HOPS):
                part = slice(h * span, (h + 1) * span)
                hops[h].wait_recv()
                value = value - dot(before[:, part], couple_hi[part, :])
        high, low = halves(value)
        stack = jnp.concatenate([high, low], axis=0)
        for h in range(HOPS):
            part = slice(h * span, (h + 1) * span)
            both = dot(stack, inverse_hi[:, part])
            solved[:, part] = (
                both[:cols] + both[cols:] + dot(high, inverse_lo[:, part])
            ).astype(BF16)
            if not last:
                hops[h].start()

    def split():
        high, low = halves(inverse[...])
        inverse_hi[...] = high
        inverse_lo[...] = low

    loads[4].wait()
    loads[5].wait()

    @pl.when(my_row == 0)
    def _():
        split()
        chain(True, n_rows == 1)

    for swap in swaps:
        swap.wait()
    near, far = pair_up(share_send, share_recv, lambda index: gathered.at[index])
    for copy in far[:1] + near:
        copy.start()

    loads[6].wait()
    loads[7].wait()

    @pl.when(my_row > 0)
    def _():
        split()
        couple_hi[...] = couple[...].astype(BF16)

    half = n_rows // 2

    @pl.when((my_row > 0) & (my_row < half))
    def _():
        chain(False, False)

    forward(near, far)

    @pl.when((my_row > 0) & (my_row >= half) & (my_row < n_rows - 1))
    def _():
        chain(False, False)

    for copy in far:
        copy.wait_recv()

    def spread(index, _):
        c = index // n_rows
        r = index % n_rows
        marks = gathered[c, r, CAP * tile : (CAP + 1) * tile, :].astype(F32)
        tiles = [gathered[c, r, s * tile : (s + 1) * tile, :] for s in range(CAP)]
        rows = [jnp.broadcast_to(marks[s : s + 1, :], (tile, blk)) for s in range(CAP)]
        base = (r * n_cols + c) * (tpd * tile)

        def gate(test):
            return jnp.where(test, 1.0, 0.0).astype(BF16)

        gates = []
        kept = []
        for s in range(CAP):
            least = [rows[s] >= float(t * per_row) for t in range(tpd + 1)]
            kept.append(
                [tiles[s] * gate(least[t] & ~least[t + 1]) for t in range(tpd)]
            )
            local = rows[s]
            for t in range(1, tpd):
                local = local - jnp.where(least[t], float(per_row), 0.0)
            gates.append([gate(local == float(j)) for j in range(per_row)])
        for t in range(tpd):
            for j in range(per_row):
                total = kept[0][t] * gates[0][j]
                for s in range(1, CAP):
                    total = total + kept[s][t] * gates[s][j]
                dense[
                    pl.ds(pl.multiple_of(base + t * tile, tile), tile), j * blk : (j + 1) * blk
                ] = total
        return 0

    lax.fori_loop(0, n_rows * n_cols, spread, 0)

    ahead = lax.broadcasted_iota(jnp.int32, (tile, group), 1)
    down = lax.broadcasted_iota(jnp.int32, (tile, group), 0)
    for i in range(tpr):
        same = ahead == slot_ref[0, i] * tile + down
        order[i * tile : (i + 1) * tile, :] = jnp.where(same, 1.0, 0.0).astype(BF16)

    @pl.when((my_row > 0) & (my_row == n_rows - 1))
    def _():
        chain(False, True)

    shares, _, wide = turned.shape

    def product(r, p):
        rows = pl.ds(pl.multiple_of(r * group + p * wide, wide), wide)
        return lax.dot_general(dense[rows, :], solved[...], NT, preferred_element_type=F32).T

    parts = []
    for p in range(shares):
        for step in range(1, n_rows):
            partial[step, p] = product(lax.rem(my_row + step, n_rows), p).astype(BF16)
            part = pltpu.make_async_remote_copy(
                src_ref=partial.at[step, p],
                dst_ref=arrived.at[step, p],
                send_sem=part_send.at[p * n_rows + step],
                recv_sem=part_recv.at[p * n_rows + step],
                device_id=row_peer(step),
                device_id_type=pl.DeviceIdType.MESH,
            )
            part.start()
            parts.append(part)

    def slab(index):
        return pl.ds(pl.multiple_of(index * cols, cols), cols)

    turns = []
    for p in range(shares):
        total = product(my_row, p)
        for step in range(1, n_rows):
            parts[p * (n_rows - 1) + step - 1].wait_recv()
            total = total + arrived[step, p].astype(F32)
        turned[p, slab(my_col), :] = total.astype(BF16)
        turn = pair_up(
            turn_send,
            turn_recv,
            lambda index, p=p: turned.at[p, slab(index)],
            p * (n_cols + 1),
        )
        for copy in turn[1][:1] + turn[0]:
            copy.start()
        turns.append(turn)
    for turn in turns:
        forward(*turn)
    total = None
    for p, turn in enumerate(turns):
        for copy in turn[1]:
            copy.wait_recv()
        moved = lax.dot_general(
            order[:, p * wide : (p + 1) * wide], turned[p], NT, preferred_element_type=F32
        )
        total = moved if total is None else total + moved
    out[...] = total.astype(BF16)

    for turn in turns:
        parts = parts + turn[0] + turn[1]
    for copy in near + far + parts:
        copy.wait_send()

    @pl.when(my_row < n_rows - 1)
    def _():
        for hop in hops:
            hop.wait_send()


def shards(
    n_rows,
    n_cols,
    rhs,
    couple_prev,
    diag_inverse,
    coupling,
    pair_block,
    pair_tile,
    pair_count,
    owner_slot,
    schur,
    surface_factor,
):
    cols, width = rhs.shape
    held, tile, blk = coupling.shape
    group = owner_slot.shape[1] * tile
    chunk = (CAP + 1) * tile
    shares = 3 if group % (3 * blk) == 0 else 1
    dma = pltpu.SemaphoreType.DMA
    vmem = pl.BlockSpec(memory_space=pltpu.VMEM)
    hbm = pl.BlockSpec(memory_space=pltpu.HBM)
    scratch = [
        pltpu.VMEM((cols, width), F32),
        pltpu.VMEM((width, width), F32),
        pltpu.VMEM((width, width), F32),
        pltpu.VMEM((held, tile, blk), BF16),
        pltpu.SMEM((held,), jnp.int32),
        pltpu.SMEM((held,), jnp.int32),
        pltpu.SMEM((1,), jnp.int32),
        pltpu.SMEM(owner_slot.shape, jnp.int32),
        pltpu.VMEM((width, width), BF16),
        pltpu.VMEM((width, width), BF16),
        pltpu.VMEM((width, width), BF16),
        pltpu.VMEM((n_rows, chunk, blk), BF16),
        pltpu.VMEM((n_cols, n_rows, chunk, blk), BF16),
        pltpu.VMEM((n_rows * group, width), BF16),
        pltpu.VMEM((group, group), BF16),
        pltpu.VMEM((cols, width), BF16),
        pltpu.VMEM((cols, width), BF16),
        pltpu.VMEM((n_rows, shares, cols, group // shares), BF16),
        pltpu.VMEM((n_rows, shares, cols, group // shares), BF16),
        pltpu.VMEM((shares, n_cols * cols, group // shares), BF16),
        dma((8,)),
        dma((n_rows,)),
        dma((n_rows,)),
        dma((n_cols + 1,)),
        dma((n_cols + 1,)),
        dma((HOPS,)),
        dma((HOPS,)),
        dma((n_rows * shares,)),
        dma((n_rows * shares,)),
        dma(((n_cols + 1) * shares,)),
        dma(((n_cols + 1) * shares,)),
    ]
    beside = 2 * (schur.size + surface_factor.size)
    rows_w = pl.pallas_call(
        functools.partial(kernel, n_rows, n_cols),
        out_shape=jax.ShapeDtypeStruct((group, n_cols * cols), BF16),
        in_specs=[hbm] * 8,
        out_specs=vmem,
        scratch_shapes=scratch,
        compiler_params=pltpu.CompilerParams(
            collective_id=0,
            has_side_effects=True,
            vmem_limit_bytes=VMEM - beside - 2**20,
        ),
        name="solve_and_route",
    )(rhs, couple_prev, diag_inverse, coupling, pair_block, pair_tile, pair_count, owner_slot)
    change = jnp.dot(rows_w, surface_factor, preferred_element_type=F32)
    return (schur.astype(F32) - change).astype(BF16)


def solution(mesh):
    placed = (
        P("col", "row"),
        P("row", None),
        P("row", None),
        P(("row", "col"), None, None),
        P(("row", "col")),
        P(("row", "col")),
        P(("row", "col")),
        P("row", None),
        P("row", "col"),
        P(None, "col"),
    )
    return jax.shard_map(
        functools.partial(shards, mesh.shape["row"], mesh.shape["col"]),
        mesh=mesh,
        in_specs=placed,
        out_specs=P("row", "col"),
        check_vma=False,
    )
```

```python
import functools

import jax
import jax.numpy as jnp
from jax import lax
from jax.experimental import pallas as pl
from jax.experimental.pallas import tpu as pltpu
from jax.sharding import PartitionSpec as P

CAP = 3
HOPS = 4
LOTS = 4
VMEM = 64 * 2**20
F32 = jnp.float32
BF16 = jnp.bfloat16
NT = (((1,), (1,)), ((), ()))


def dot(left, right):
    return jnp.dot(left, right, preferred_element_type=F32)


def halves(value):
    high = value.astype(BF16)
    return high, (value - high.astype(F32)).astype(BF16)


def kernel(
    n_rows,
    n_cols,
    rhs_hbm,
    couple_hbm,
    inverse_hbm,
    coupling_hbm,
    block_hbm,
    tile_hbm,
    count_hbm,
    slot_hbm,
    out,
    rhs,
    couple,
    inverse,
    coupling,
    block_ref,
    tile_ref,
    count_ref,
    slot_ref,
    couple_hi,
    inverse_hi,
    inverse_lo,
    chunks,
    gathered,
    dense,
    order,
    solved,
    before,
    partial,
    arrived,
    turned,
    load_sem,
    swap_send,
    swap_recv,
    share_send,
    share_recv,
    hop_send,
    hop_recv,
    part_send,
    part_recv,
    turn_send,
    turn_recv,
):
    my_row = lax.axis_index("row")
    my_col = lax.axis_index("col")
    cols, width = rhs.shape
    held, tile, blk = coupling.shape
    per_row = width // blk
    tpr = slot_ref.shape[1]
    tpd = tpr // n_cols
    group = tpr * tile

    pairs = [
        (block_hbm, block_ref),
        (tile_hbm, tile_ref),
        (count_hbm, count_ref),
        (coupling_hbm, coupling),
        (rhs_hbm, rhs),
        (slot_hbm, slot_ref),
    ]
    lots = [slice(i * (width // LOTS), (i + 1) * (width // LOTS)) for i in range(LOTS)]
    pairs += [(inverse_hbm.at[lot], inverse.at[lot]) for lot in lots]
    pairs += [(couple_hbm.at[lot], couple.at[lot]) for lot in lots]
    loads = [
        pltpu.make_async_copy(source, target, load_sem.at[i])
        for i, (source, target) in enumerate(pairs)
    ]
    for load in loads:
        load.start()

    def row_peer(step):
        return {"row": lax.rem(my_row + step, n_rows)}

    def col_peer(step):
        return {"col": lax.rem(my_col + step, n_cols)}

    pair = 2 if n_cols % 2 == 0 else 1
    line = n_cols // pair

    def pair_up(send, recv, block, base=0):
        lane = lax.rem(my_col, pair)
        major = my_col // pair
        near, far = [], []

        def push(index, target, number):
            return pltpu.make_async_remote_copy(
                src_ref=block(index),
                dst_ref=block(index),
                send_sem=send.at[base + number],
                recv_sem=recv.at[base + number],
                device_id={"col": target},
                device_id_type=pl.DeviceIdType.MESH,
            )

        for step in range(1, line):
            near.append(push(my_col, lax.rem(major + step, line) * pair + lane, step))
        for step in range(line):
            source = lax.rem(major + line - step, line) * pair + lane
            if pair > 1:
                far.append(push(source, major * pair + 1 - lane, line + step))
        return near, far

    def forward(near, far):
        for step in range(1, line):
            near[step - 1].wait_recv()
            for copy in far[step : step + 1]:
                copy.start()

    barrier = pltpu.get_barrier_semaphore()
    for step in range(1, n_rows):
        pl.semaphore_signal(
            barrier, inc=1, device_id=row_peer(step), device_id_type=pl.DeviceIdType.MESH
        )
    for step in range(1, n_cols):
        pl.semaphore_signal(
            barrier, inc=1, device_id=col_peer(step), device_id_type=pl.DeviceIdType.MESH
        )

    for load in loads[:4]:
        load.wait()

    count = count_ref[0]
    keys, codes = [], []
    sources = []
    for k in range(held):
        block = block_ref[k]
        source = lax.div(block, per_row)
        rank = jnp.int32(0)
        for j in range(k):
            rank = rank + jnp.where(sources[j] == source, 1, 0)
        sources.append(jnp.where(k < count, source, -1))
        keys.append(jnp.where(k < count, source * CAP + rank, -1))
        codes.append(tile_ref[k] * per_row + block - source * per_row)
    lines = lax.broadcasted_iota(jnp.int32, (tile, blk), 0)
    for r in range(n_rows):
        marks = jnp.full((tile, blk), -1, jnp.int32)
        for s in range(CAP):
            place, code = jnp.int32(0), jnp.int32(-1)
            for k in range(held):
                hit = keys[k] == r * CAP + s
                place = jnp.where(hit, k, place)
                code = jnp.where(hit, codes[k], code)
            chunks[r, s * tile : (s + 1) * tile, :] = coupling[place]
            marks = jnp.where(lines == s, code, marks)
        chunks[r, CAP * tile : (CAP + 1) * tile, :] = marks.astype(F32).astype(BF16)
    gathered[my_col, my_row] = chunks[my_row]

    pl.semaphore_wait(barrier, n_rows + n_cols - 2)

    swaps = []
    for step in range(1, n_rows):
        swap = pltpu.make_async_remote_copy(
            src_ref=chunks.at[lax.rem(my_row + step, n_rows)],
            dst_ref=gathered.at[my_col, my_row],
            send_sem=swap_send.at[step],
            recv_sem=swap_recv.at[step],
            device_id=row_peer(step),
            device_id_type=pl.DeviceIdType.MESH,
        )
        swap.start()
        swaps.append(swap)

    span = width // HOPS
    hops = []
    for h in range(HOPS):
        ahead = slice(h * span, (h + 1) * span)
        hops.append(
            pltpu.make_async_remote_copy(
                src_ref=solved.at[:, ahead],
                dst_ref=before.at[:, ahead],
                send_sem=hop_send.at[h],
                recv_sem=hop_recv.at[h],
                device_id=row_peer(1),
                device_id_type=pl.DeviceIdType.MESH,
            )
        )

    def chain(first, last):
        value = rhs[...]
        if not first:
            for h in range(HOPS):
                part = slice(h * span, (h + 1) * span)
                hops[h].wait_recv()
                value = value - dot(before[:, part], couple_hi[part, :])
        high, low = halves(value)
        stack = jnp.concatenate([high, low], axis=0)
        for h in range(HOPS):
            part = slice(h * span, (h + 1) * span)
            both = dot(stack, inverse_hi[:, part])
            solved[:, part] = (
                both[:cols] + both[cols:] + dot(high, inverse_lo[:, part])
            ).astype(BF16)
            if not last:
                hops[h].start()

    def split():
        for i, lot in enumerate(lots):
            loads[6 + i].wait()
            high, low = halves(inverse[lot, :])
            inverse_hi[lot, :] = high
            inverse_lo[lot, :] = low

    loads[4].wait()
    loads[5].wait()

    @pl.when(my_row == 0)
    def _():
        split()
        chain(True, n_rows == 1)

    for swap in swaps:
        swap.wait()
    near, far = pair_up(share_send, share_recv, lambda index: gathered.at[index])
    for copy in far[:1] + near:
        copy.start()

    @pl.when(my_row > 0)
    def _():
        split()
        for i, lot in enumerate(lots):
            loads[6 + LOTS + i].wait()
            couple_hi[lot, :] = couple[lot, :].astype(BF16)

    half = n_rows // 2

    @pl.when((my_row > 0) & (my_row < half))
    def _():
        chain(False, False)

    forward(near, far)

    @pl.when((my_row > 0) & (my_row >= half) & (my_row < n_rows - 1))
    def _():
        chain(False, False)

    for copy in far:
        copy.wait_recv()

    def spread(index, _):
        c = index // n_rows
        r = index % n_rows
        marks = gathered[c, r, CAP * tile : (CAP + 1) * tile, :].astype(F32)
        tiles = [gathered[c, r, s * tile : (s + 1) * tile, :] for s in range(CAP)]
        rows = [jnp.broadcast_to(marks[s : s + 1, :], (tile, blk)) for s in range(CAP)]
        base = (r * n_cols + c) * (tpd * tile)

        def gate(test):
            return jnp.where(test, 1.0, 0.0).astype(BF16)

        gates = []
        kept = []
        for s in range(CAP):
            least = [rows[s] >= float(t * per_row) for t in range(tpd + 1)]
            kept.append(
                [tiles[s] * gate(least[t] & ~least[t + 1]) for t in range(tpd)]
            )
            local = rows[s]
            for t in range(1, tpd):
                local = local - jnp.where(least[t], float(per_row), 0.0)
            gates.append([gate(local == float(j)) for j in range(per_row)])
        for t in range(tpd):
            for j in range(per_row):
                total = kept[0][t] * gates[0][j]
                for s in range(1, CAP):
                    total = total + kept[s][t] * gates[s][j]
                dense[
                    pl.ds(pl.multiple_of(base + t * tile, tile), tile), j * blk : (j + 1) * blk
                ] = total
        return 0

    @pl.when(my_row == 0)
    def _():
        for load in loads[6 + LOTS :]:
            load.wait()

    lax.fori_loop(0, n_rows * n_cols, spread, 0)

    ahead = lax.broadcasted_iota(jnp.int32, (tile, group), 1)
    down = lax.broadcasted_iota(jnp.int32, (tile, group), 0)
    for i in range(tpr):
        same = ahead == slot_ref[0, i] * tile + down
        order[i * tile : (i + 1) * tile, :] = jnp.where(same, 1.0, 0.0).astype(BF16)

    @pl.when((my_row > 0) & (my_row == n_rows - 1))
    def _():
        chain(False, True)

    shares, _, wide = turned.shape

    def product(r, p):
        rows = pl.ds(pl.multiple_of(r * group + p * wide, wide), wide)
        return lax.dot_general(dense[rows, :], solved[...], NT, preferred_element_type=F32).T

    parts = []
    for p in range(shares):
        for step in range(1, n_rows):
            partial[step, p] = product(lax.rem(my_row + step, n_rows), p).astype(BF16)
            part = pltpu.make_async_remote_copy(
                src_ref=partial.at[step, p],
                dst_ref=arrived.at[step, p],
                send_sem=part_send.at[p * n_rows + step],
                recv_sem=part_recv.at[p * n_rows + step],
                device_id=row_peer(step),
                device_id_type=pl.DeviceIdType.MESH,
            )
            part.start()
            parts.append(part)

    def slab(index):
        return pl.ds(pl.multiple_of(index * cols, cols), cols)

    turns = []
    for p in range(shares):
        total = product(my_row, p)
        for step in range(1, n_rows):
            parts[p * (n_rows - 1) + step - 1].wait_recv()
            total = total + arrived[step, p].astype(F32)
        turned[p, slab(my_col), :] = total.astype(BF16)
        turn = pair_up(
            turn_send,
            turn_recv,
            lambda index, p=p: turned.at[p, slab(index)],
            p * (n_cols + 1),
        )
        for copy in turn[1][:1] + turn[0]:
            copy.start()
        turns.append(turn)
    for turn in turns:
        forward(*turn)
    total = None
    for p, turn in enumerate(turns):
        for copy in turn[1]:
            copy.wait_recv()
        moved = lax.dot_general(
            order[:, p * wide : (p + 1) * wide], turned[p], NT, preferred_element_type=F32
        )
        total = moved if total is None else total + moved
    out[...] = total.astype(BF16)

    for turn in turns:
        parts = parts + turn[0] + turn[1]
    for copy in near + far + parts:
        copy.wait_send()

    @pl.when(my_row < n_rows - 1)
    def _():
        for hop in hops:
            hop.wait_send()


def shards(
    n_rows,
    n_cols,
    rhs,
    couple_prev,
    diag_inverse,
    coupling,
    pair_block,
    pair_tile,
    pair_count,
    owner_slot,
    schur,
    surface_factor,
):
    cols, width = rhs.shape
    held, tile, blk = coupling.shape
    group = owner_slot.shape[1] * tile
    chunk = (CAP + 1) * tile
    shares = 3 if group % (3 * blk) == 0 else 1
    dma = pltpu.SemaphoreType.DMA
    vmem = pl.BlockSpec(memory_space=pltpu.VMEM)
    hbm = pl.BlockSpec(memory_space=pltpu.HBM)
    scratch = [
        pltpu.VMEM((cols, width), F32),
        pltpu.VMEM((width, width), F32),
        pltpu.VMEM((width, width), F32),
        pltpu.VMEM((held, tile, blk), BF16),
        pltpu.SMEM((held,), jnp.int32),
        pltpu.SMEM((held,), jnp.int32),
        pltpu.SMEM((1,), jnp.int32),
        pltpu.SMEM(owner_slot.shape, jnp.int32),
        pltpu.VMEM((width, width), BF16),
        pltpu.VMEM((width, width), BF16),
        pltpu.VMEM((width, width), BF16),
        pltpu.VMEM((n_rows, chunk, blk), BF16),
        pltpu.VMEM((n_cols, n_rows, chunk, blk), BF16),
        pltpu.VMEM((n_rows * group, width), BF16),
        pltpu.VMEM((group, group), BF16),
        pltpu.VMEM((cols, width), BF16),
        pltpu.VMEM((cols, width), BF16),
        pltpu.VMEM((n_rows, shares, cols, group // shares), BF16),
        pltpu.VMEM((n_rows, shares, cols, group // shares), BF16),
        pltpu.VMEM((shares, n_cols * cols, group // shares), BF16),
        dma((6 + 2 * LOTS,)),
        dma((n_rows,)),
        dma((n_rows,)),
        dma((n_cols + 1,)),
        dma((n_cols + 1,)),
        dma((HOPS,)),
        dma((HOPS,)),
        dma((n_rows * shares,)),
        dma((n_rows * shares,)),
        dma(((n_cols + 1) * shares,)),
        dma(((n_cols + 1) * shares,)),
    ]
    beside = 2 * (schur.size + surface_factor.size)
    rows_w = pl.pallas_call(
        functools.partial(kernel, n_rows, n_cols),
        out_shape=jax.ShapeDtypeStruct((group, n_cols * cols), BF16),
        in_specs=[hbm] * 8,
        out_specs=vmem,
        scratch_shapes=scratch,
        compiler_params=pltpu.CompilerParams(
            collective_id=0,
            has_side_effects=True,
            vmem_limit_bytes=VMEM - beside - 2**20,
        ),
        name="solve_and_route",
    )(rhs, couple_prev, diag_inverse, coupling, pair_block, pair_tile, pair_count, owner_slot)
    change = jnp.dot(rows_w, surface_factor, preferred_element_type=F32)
    return (schur.astype(F32) - change).astype(BF16)


def solution(mesh):
    placed = (
        P("col", "row"),
        P("row", None),
        P("row", None),
        P(("row", "col"), None, None),
        P(("row", "col")),
        P(("row", "col")),
        P(("row", "col")),
        P("row", None),
        P("row", "col"),
        P(None, "col"),
    )
    return jax.shard_map(
        functools.partial(shards, mesh.shape["row"], mesh.shape["col"]),
        mesh=mesh,
        in_specs=placed,
        out_specs=P("row", "col"),
        check_vma=False,
    )
```
